768 devices in a mesh: pair: 64 (over x, y, core), virt: 12 (over z).
Axes of the slice: x: 4, y: 8, z: 12, core: 2. Of those that a mesh axis runs over, the one named last changes fastest.
Arguments:
- amplitudes: float32 [64, 12288, 256], P('pair', 'virt'), may hold values from -4 to 4
- source: float32 [64, 12288, 256], P('pair', 'virt'), may hold values from -12 to 12
- diag_block: float32 [12288, 1024], P('virt'), may hold values from -0.1875 to 0.1875
- edge_low: float32 [3072, 256], P('virt'), may hold values from -0.375 to 0.375
- edge_high: float32 [3072, 256], P('virt'), may hold values from -0.375 to 0.375
- hole_coupling: float32 [64, 64], replicated, may hold values from -0.75 to 0.75
- pair_energy: float32 [64], replicated, may hold values from -3 to -1
- virt_energy: float32 [12288], replicated, may hold values from 1 to 4
- column_tiles: int32 [2], replicated, may hold values from 0 to 95, as said below
Outputs:
- updated: float32 [64, 12288, 256], P('pair', 'virt')
The draws below stay inside these ranges and needn't reach their ends.
Inputs may be any that keep to these rules, and one draw needn't show every extreme that they name: `column_tiles`: 2 distinct tile numbers; the last entry is always the highest tile, 95.
All inputs are finite; a program needn't handle non-finite values.
Results may differ from the reference program's by a relative error of at most 0.0003.
Values sent between devices are 32-bit elements; how exact they have to be, the bound alone decides.
No kernel may reach another device: no remote copies, remote signals or barrier semaphores. Data moves between devices by JAX's collectives and lax.ppermute only.
A program may use at most 64 MiB of HBM per device.

```python
import jax
import jax.numpy as jnp
from jax import lax

TW = 128
VT_DEV = 8
NZ = 2
H = 256
ITERS = 2
VB = 1024
V = 12288
NB = 256
PAIRS = 64
N_VIRT = 12


def draw_column_tiles(key, part):
    key = jax.random.fold_in(key, 11)
    chosen = jax.random.permutation(key, V // TW - 1)[:NZ - 1]
    highest = jnp.full((1,), V // TW - 1, dtype=jnp.int32)
    return jnp.concatenate([chosen.astype(jnp.int32), highest])


def levels(rng, dims, split, least, top_value):
    def one(position, blocks):
        draws = jax.random.uniform(jax.random.fold_in(jax.random.fold_in(rng, 6), position), (blocks,), jnp.float32, least / len(split), top_value / len(split))
        return jnp.repeat(jnp.exp(draws), dims[position] // blocks).reshape((-1,) + (1,) * (len(dims) - position - 1))

    gain = one(*split[0])
    for cut in split[1:]:
        gain = gain * one(*cut)
    return gain


def noise(own_key, dims, scale, limit, cuts=(), kind=jnp.bfloat16):
    level = levels(own_key, dims, cuts, -0.22, 0.18) if cuts else 1.0
    drawn = jax.random.normal(own_key, dims, jnp.float32) * scale * level
    return jnp.minimum(jnp.maximum(drawn, -limit), limit).astype(kind)


def setup_inputs(seed: int = 0) -> dict:
    key_list = jax.random.split(jax.random.key(seed), 10)
    return {
        "amplitudes": noise(key_list[0], (PAIRS, V, NB), 0.5, 4.0, ((0, 64), (1, 12)), jnp.float32),
        "source": noise(key_list[1], (PAIRS, V, NB), 3.0, 12.0, ((0, 64), (1, 12)), jnp.float32),
        "diag_block": noise(key_list[2], (V, VB), VB ** -0.5, 0.1875, ((0, 12),), jnp.float32),
        "edge_low": noise(key_list[3], (H * N_VIRT, H), H ** -0.5, 0.375, ((0, 12),), jnp.float32),
        "edge_high": noise(key_list[4], (H * N_VIRT, H), H ** -0.5, 0.375, ((0, 12),), jnp.float32),
        "hole_coupling": noise(key_list[5], (PAIRS, PAIRS), PAIRS ** -0.5, 0.75, (), jnp.float32),
        "pair_energy": jnp.clip(jax.random.uniform(key_list[6], (PAIRS,), jnp.float32, -3.0, -1.0), -3.0, -1.0),
        "virt_energy": jnp.clip(jax.random.uniform(key_list[7], (V,), jnp.float32, 1.0, 4.0), 1.0, 4.0),
        "column_tiles": draw_column_tiles(jax.random.fold_in(key_list[9], 71), 0),
    }


def reference(amplitudes, source, diag_block, edge_low, edge_high, hole_coupling, pair_energy, virt_energy, column_tiles):
    exact = lax.Precision.HIGHEST
    rows = VT_DEV * TW
    blocks = V // rows
    width = H
    index = (column_tiles[:, None] * TW + jnp.arange(TW, dtype=jnp.int32)[None, :]).reshape(-1).astype(jnp.int32)
    denom = virt_energy[None, :, None] + virt_energy[index][None, None, :] - pair_energy[:, None, None]

    def band(field):
        def one_block(block):
            start = block * rows
            local = lax.dynamic_slice_in_dim(field, start, rows, 1)
            diag = lax.dynamic_slice_in_dim(diag_block, start, rows, 0)
            lower_w = lax.dynamic_slice_in_dim(edge_low, block * width, width, 0)
            upper_w = lax.dynamic_slice_in_dim(edge_high, block * width, width, 0)
            before = lax.dynamic_slice_in_dim(field, jnp.maximum(start - width, 0).astype(jnp.int32), width, 1)
            before = before * (block > 0).astype(jnp.float32)
            after = lax.dynamic_slice_in_dim(field, jnp.minimum(start + rows, V - width).astype(jnp.int32), width, 1)
            after = after * (block < blocks - 1).astype(jnp.float32)
            out = jnp.einsum("rc,pcn->prn", diag, local, precision=exact)
            out = out.at[:, :width].add(jnp.einsum("rc,pcn->prn", lower_w, before, precision=exact))
            out = out.at[:, rows - width:].add(jnp.einsum("rc,pcn->prn", upper_w, after, precision=exact))
            return out

        parts = lax.map(one_block, jnp.arange(blocks, dtype=jnp.int32))
        return jnp.transpose(parts, (1, 0, 2, 3)).reshape(field.shape)

    field = amplitudes
    for step in range(ITERS):
        hole = jnp.einsum("pq,qrn->prn", hole_coupling, field, precision=exact)
        field = (source + band(field) + hole) / denom
    return field
```

```python
import functools

import jax
import jax.numpy as jnp
from jax import lax
from jax.experimental import pallas as pl
from jax.experimental.pallas import tpu as pltpu
from jax.sharding import PartitionSpec as P

TW = 128
ITERS = 2
BF = jnp.bfloat16
F32 = jnp.float32
VMEM = pl.BlockSpec(memory_space=pltpu.VMEM)
LIMIT = 40 * 1024 * 1024


def split(x):
    hi = x.astype(BF)
    return hi, (x - hi.astype(F32)).astype(BF)


def dot_nt(x, w):
    return lax.dot_general(x, w, (((1,), (1,)), ((), ())), preferred_element_type=F32)


def dot_nn(x, w):
    return jnp.dot(x, w, preferred_element_type=F32)


def three(dot, xh, xl, wh, wl):
    return dot(xh, wh) + (dot(xl, wh) + dot(xh, wl))


def pack_kernel(a_ref, s_ref, o_ref):
    k = pl.program_id(0)
    nk = pl.num_programs(0)
    for t in range(a_ref.shape[1] // TW):
        cols = slice(t * TW, (t + 1) * TW)
        base = t * TW * 2 * nk
        o_ref[pl.ds(base + k, TW, stride=2 * nk), :] = a_ref[:, cols].T
        o_ref[pl.ds(base + nk + k, TW, stride=2 * nk), :] = s_ref[:, cols].T


def pack(a, s):
    rows, cols = a.shape
    nk = rows // TW
    return pl.pallas_call(
        pack_kernel,
        grid=(nk,),
        in_specs=[pl.BlockSpec((TW, cols), lambda k: (k, 0))] * 2,
        out_specs=pl.BlockSpec((cols * 2 * nk, TW), lambda k: (0, 0)),
        out_shape=jax.ShapeDtypeStruct((cols * 2 * nk, TW), F32),
        compiler_params=pltpu.CompilerParams(vmem_limit_bytes=LIMIT),
        name="pack",
    )(a, s)


def unpack_kernel(u_ref, o_ref):
    k = pl.program_id(0)
    nk = pl.num_programs(0)
    for t in range(o_ref.shape[1] // TW):
        base = t * TW * nk
        o_ref[:, t * TW : (t + 1) * TW] = u_ref[pl.ds(base + k, TW, stride=nk), :].T


def unpack(u, rows, cols):
    nk = rows // TW
    return pl.pallas_call(
        unpack_kernel,
        grid=(nk,),
        in_specs=[pl.BlockSpec((cols * nk, TW), lambda k: (0, 0))],
        out_specs=pl.BlockSpec((TW, cols), lambda k: (k, 0)),
        out_shape=jax.ShapeDtypeStruct((rows, cols), F32),
        compiler_params=pltpu.CompilerParams(vmem_limit_bytes=LIMIT),
        name="unpack",
    )(u)


def prep_kernel(share, d_ref, l_ref, dh_ref, dl_ref, kh_ref, kl_ref):
    dh_ref[...], dl_ref[...] = split(d_ref[...])
    pairs = l_ref.shape[0]
    size = pairs * share
    spread = (
        lax.broadcasted_iota(jnp.int32, (size, pairs), 0) // share
        == lax.broadcasted_iota(jnp.int32, (size, pairs), 1)
    ).astype(F32).astype(BF)
    same = (
        lax.broadcasted_iota(jnp.int32, (size, size), 0) % share
        == lax.broadcasted_iota(jnp.int32, (size, size), 1) % share
    )
    for part, ref in zip(split(l_ref[...]), (kh_ref, kl_ref)):
        tall = dot_nn(spread, part).astype(BF)
        wide = dot_nt(tall, spread)
        ref[...] = jnp.where(same, wide, 0.0).astype(BF)


def prep(d, l, share):
    rows = d.shape[0]
    size = l.shape[0] * share
    return pl.pallas_call(
        functools.partial(prep_kernel, share),
        in_specs=[VMEM] * 2,
        out_specs=[VMEM] * 4,
        out_shape=[jax.ShapeDtypeStruct((rows, rows), BF)] * 2
        + [jax.ShapeDtypeStruct((size, size), BF)] * 2,
        compiler_params=pltpu.CompilerParams(vmem_limit_bytes=LIMIT),
        cost_estimate=pl.CostEstimate(
            flops=8 * rows * rows, bytes_accessed=8 * rows * rows, transcendentals=0
        ),
        name="prep",
    )(d, l)


def edges_kernel(nk, p_ref, first_ref, last_ref):
    lines = first_ref.shape[0]
    tiles = first_ref.shape[1] // TW
    for j in range(tiles):
        cols = slice(j * TW, (j + 1) * TW)
        first_ref[:, cols] = p_ref[pl.ds(j, lines, stride=2 * nk), :]
        last_ref[:, cols] = p_ref[pl.ds(nk - tiles + j, lines, stride=2 * nk), :]


def edges(p, nk, width):
    lines = p.shape[0] // (2 * nk)
    return pl.pallas_call(
        functools.partial(edges_kernel, nk),
        in_specs=[VMEM],
        out_specs=[VMEM] * 2,
        out_shape=[jax.ShapeDtypeStruct((lines, width), F32)] * 2,
        compiler_params=pltpu.CompilerParams(vmem_limit_bytes=LIMIT),
        name="edges",
    )(p)


def inner_kernel(nk, packed, *refs):
    if packed:
        p_ref, dh_ref, dl_ref, kh_ref, kl_ref, o_ref, xh_ref, xl_ref = refs
    else:
        f_ref, p_ref, dh_ref, dl_ref, kh_ref, kl_ref, o_ref, xh_ref, xl_ref = refs
    lines = o_ref.shape[0]
    for k in range(nk):
        cols = slice(k * TW, (k + 1) * TW)
        part = p_ref[pl.ds(k, lines, stride=2 * nk), :] if packed else f_ref[:, cols]
        xh_ref[:, cols], xl_ref[:, cols] = split(part)
    kh = kh_ref[...]
    kl = kl_ref[...]
    wide = 2 * TW
    for c in range(nk // 2):
        cols = slice(c * wide, (c + 1) * wide)
        out = three(dot_nt, xh_ref[...], xl_ref[...], dh_ref[cols, :], dl_ref[cols, :])
        out += three(dot_nn, kh, kl, xh_ref[:, cols], xl_ref[:, cols])
        for j in range(2):
            k = 2 * c + j
            o_ref[:, k * TW : (k + 1) * TW] = (
                out[:, j * TW : (j + 1) * TW] + p_ref[pl.ds(nk + k, lines, stride=2 * nk), :]
            )


def inner(field, p, parts, nk):
    lines = p.shape[0] // (2 * nk)
    rows = nk * TW
    packed = field is None
    args = ([] if packed else [field]) + [p, *parts]
    return pl.pallas_call(
        functools.partial(inner_kernel, nk, packed),
        in_specs=[VMEM] * len(args),
        out_specs=VMEM,
        out_shape=jax.ShapeDtypeStruct((lines, rows), F32),
        scratch_shapes=[pltpu.VMEM((lines, rows), BF)] * 2,
        compiler_params=pltpu.CompilerParams(vmem_limit_bytes=LIMIT),
        cost_estimate=pl.CostEstimate(
            flops=6 * lines * rows * (rows + lines),
            bytes_accessed=4 * rows * rows + 16 * lines * rows,
            transcendentals=0,
        ),
        name="inner",
    )(*args)


def finish_kernel(nk, last_step, sum_ref, before_ref, after_ref, low_ref, high_ref, row_ref, col_ref, pair_ref, *outs):
    lines, rows = sum_ref.shape
    width = low_ref.shape[0]
    low = three(dot_nt, *split(before_ref[...]), *split(low_ref[...]))
    high = three(dot_nt, *split(after_ref[...]), *split(high_ref[...]))
    col = col_ref[...]
    pair = pair_ref[...]
    for k in range(nk):
        cols = slice(k * TW, (k + 1) * TW)
        x = sum_ref[:, cols]
        at = k * TW
        if at < width:
            x += low[:, at : at + TW]
        at -= rows - width
        if at >= 0:
            x += high[:, at : at + TW]
        x = x / (row_ref[:, cols] + col - pair)
        if last_step:
            outs[0][pl.ds(k, lines, stride=nk), :] = x
        else:
            outs[0][:, cols] = x
            if k * TW < width:
                outs[1][:, cols] = x
            if at >= 0:
                outs[2][:, at : at + TW] = x


def finish(total, before, after, low, high, energies, nk, last_step):
    lines, rows = total.shape
    width = low.shape[0]
    edge = jax.ShapeDtypeStruct((lines, width), F32)
    if last_step:
        shapes = [jax.ShapeDtypeStruct((lines * nk, TW), F32)]
    else:
        shapes = [jax.ShapeDtypeStruct((lines, rows), F32), edge, edge]
    args = [total, before, after, low, high, *energies]
    return pl.pallas_call(
        functools.partial(finish_kernel, nk, last_step),
        in_specs=[VMEM] * len(args),
        out_specs=[VMEM] * len(shapes),
        out_shape=shapes,
        compiler_params=pltpu.CompilerParams(vmem_limit_bytes=LIMIT),
        name="finish",
    )(*args)


def exchange(first, last):
    count = lax.axis_size("virt")
    up = [(i, i + 1) for i in range(count - 1)]
    down = [(j, i) for i, j in up]
    before = lax.ppermute(last, "virt", up)
    after = lax.ppermute(first, "virt", down)
    return before, after


def local(
    amplitudes,
    source,
    diag_block,
    edge_low,
    edge_high,
    hole_coupling,
    pair_energy,
    virt_energy,
    column_tiles,
):
    rows, cols = amplitudes.shape[1:]
    width = edge_low.shape[0]
    pairs = pair_energy.shape[0]
    share = cols // pairs
    nk = rows // TW

    packed = pack(amplitudes[0], source[0]).reshape(pairs, share * 2 * nk, TW)
    held = lax.all_to_all(packed, "pair", split_axis=0, concat_axis=0, tiled=True)
    held = held.reshape(cols * 2 * nk, TW)

    parts = prep(diag_block, hole_coupling, share)
    row = lax.dynamic_slice_in_dim(virt_energy, lax.axis_index("virt") * rows, rows)[None, :]
    start = lax.axis_index("pair") * share
    tile = lax.dynamic_index_in_dim(column_tiles, start // TW, keepdims=False)
    kept = lax.dynamic_slice_in_dim(virt_energy, tile * TW + start % TW, share)
    col = jnp.broadcast_to(kept[None, :], (pairs, share)).reshape(-1, 1)
    own = jnp.broadcast_to(pair_energy[:, None], (pairs, share)).reshape(-1, 1)
    energies = (row, col, own)

    first, last = edges(held, nk, width)
    field = None
    for step in range(ITERS):
        before, after = exchange(first, last)
        total = inner(field, held, parts, nk)
        out = finish(total, before, after, edge_low, edge_high, energies, nk, step == ITERS - 1)
        if step < ITERS - 1:
            field, first, last = out
    back = lax.all_to_all(
        out[0].reshape(pairs, share * nk, TW), "pair", split_axis=0, concat_axis=0, tiled=True
    )
    return unpack(back.reshape(cols * nk, TW), rows, cols)[None]


def solution(mesh):
    in_specs = (
        P("pair", "virt", None),
        P("pair", "virt", None),
        P("virt", None),
        P("virt", None),
        P("virt", None),
        P(),
        P(),
        P(),
        P(),
    )
    out_specs = P("pair", "virt", None)
    return jax.shard_map(local, mesh=mesh, in_specs=in_specs, out_specs=out_specs, check_vma=False)
```

```python
import functools

import jax
import jax.numpy as jnp
from jax import lax
from jax.experimental import pallas as pl
from jax.experimental.pallas import tpu as pltpu
from jax.sharding import PartitionSpec as P

TW = 128
BF = jnp.bfloat16
F32 = jnp.float32
VMEM = pl.BlockSpec(memory_space=pltpu.VMEM)
HBM = pl.BlockSpec(memory_space=pltpu.HBM)
LIMIT = 16 * 1024 * 1024


def split(x):
    hi = x.astype(BF)
    return hi, (x - hi.astype(F32)).astype(BF)


def dot_nt(x, w):
    return lax.dot_general(x, w, (((1,), (1,)), ((), ())), preferred_element_type=F32)


def dot_nn(x, w):
    return jnp.dot(x, w, preferred_element_type=F32)


def three(dot, xh, xl, wh, wl):
    return dot(xh, wh) + (dot(xl, wh) + dot(xh, wl))


def pack_kernel(a_hbm, s_hbm, o_hbm, a_ref, s_ref, o_ref, in_sems, out_sems):
    rows, cols = a_ref.shape
    nk = rows // TW
    arrays = ((a_hbm, a_ref), (s_hbm, s_ref))
    piece = rows // 2
    copies = {}
    for t in range(cols // TW):
        for h in range(2):
            for i, (src, dst) in enumerate(arrays):
                here = (slice(h * piece, (h + 1) * piece), slice(t * TW, (t + 1) * TW))
                copies[t, h, i] = pltpu.make_async_copy(src.at[here], dst.at[here], in_sems.at[t, h, i])
                copies[t, h, i].start()
    length = TW * 2 * nk
    part = length // 4
    sent = []
    for t in range(cols // TW):
        for h in range(2):
            for i, (_, ref) in enumerate(arrays):
                copies[t, h, i].wait()
                for k in range(h * nk // 2, (h + 1) * nk // 2):
                    block = ref[k * TW : (k + 1) * TW, t * TW : (t + 1) * TW]
                    o_ref[pl.ds(t * length + i * nk + k, TW, stride=2 * nk), :] = block.T
        for j in range(4):
            here = slice(t * length + j * part, t * length + (j + 1) * part)
            copy = pltpu.make_async_copy(o_ref.at[here, :], o_hbm.at[here, :], out_sems.at[t, j])
            copy.start()
            sent.append(copy)
    for copy in sent:
        copy.wait()


def pack(a, s):
    rows, cols = a.shape
    nk = rows // TW
    size = (cols * 2 * nk, TW)
    return pl.pallas_call(
        pack_kernel,
        in_specs=[HBM] * 2,
        out_specs=HBM,
        out_shape=jax.ShapeDtypeStruct(size, F32),
        scratch_shapes=[pltpu.VMEM((rows, cols), F32)] * 2
        + [
            pltpu.VMEM(size, F32),
            pltpu.SemaphoreType.DMA((cols // TW, 2, 2)),
            pltpu.SemaphoreType.DMA((cols // TW, 4)),
        ],
        compiler_params=pltpu.CompilerParams(vmem_limit_bytes=60 * 1024 * 1024),
        name="pack",
    )(a, s)


def unpack_kernel(u_ref, o_hbm, o_ref, sems):
    rows, cols = o_ref.shape
    nk = rows // TW
    copies = []
    for k in range(nk):
        for t in range(cols // TW):
            block = u_ref[pl.ds(t * TW * nk + k, TW, stride=nk), :]
            o_ref[k * TW : (k + 1) * TW, t * TW : (t + 1) * TW] = block.T
        here = slice(k * TW, (k + 1) * TW)
        copy = pltpu.make_async_copy(o_ref.at[here, :], o_hbm.at[here, :], sems.at[k])
        copy.start()
        copies.append(copy)
    for copy in copies:
        copy.wait()


def unpack(u, rows, cols):
    nk = rows // TW
    return pl.pallas_call(
        unpack_kernel,
        in_specs=[VMEM],
        out_specs=HBM,
        out_shape=jax.ShapeDtypeStruct((rows, cols), F32),
        scratch_shapes=[pltpu.VMEM((rows, cols), F32), pltpu.SemaphoreType.DMA((nk,))],
        compiler_params=pltpu.CompilerParams(vmem_limit_bytes=LIMIT),
        name="unpack",
    )(u)


def prep_kernel(share, d_ref, l_ref, d2_ref, kh_ref, kl_ref):
    d2_ref[0], d2_ref[1] = split(d_ref[...])
    pairs = l_ref.shape[0]
    size = pairs * share
    spread = (
        lax.broadcasted_iota(jnp.int32, (size, pairs), 0) // share
        == lax.broadcasted_iota(jnp.int32, (size, pairs), 1)
    ).astype(F32).astype(BF)
    same = (
        lax.broadcasted_iota(jnp.int32, (size, size), 0) % share
        == lax.broadcasted_iota(jnp.int32, (size, size), 1) % share
    )
    for part, ref in zip(split(l_ref[...]), (kh_ref, kl_ref)):
        tall = dot_nn(spread, part).astype(BF)
        wide = dot_nt(tall, spread)
        ref[...] = jnp.where(same, wide, 0.0).astype(BF)


def prep(d, l, share):
    rows = d.shape[0]
    size = l.shape[0] * share
    return pl.pallas_call(
        functools.partial(prep_kernel, share),
        in_specs=[VMEM] * 2,
        out_specs=[VMEM] * 3,
        out_shape=[jax.ShapeDtypeStruct((2, rows, rows), BF)]
        + [jax.ShapeDtypeStruct((size, size), BF)] * 2,
        compiler_params=pltpu.CompilerParams(vmem_limit_bytes=LIMIT),
        cost_estimate=pl.CostEstimate(
            flops=8 * rows * rows, bytes_accessed=8 * rows * rows, transcendentals=0
        ),
        name="prep",
    )(d, l)


def edges_kernel(nk, p_ref, first_ref, last_ref):
    lines = first_ref.shape[0]
    tiles = first_ref.shape[1] // TW
    for j in range(tiles):
        cols = slice(j * TW, (j + 1) * TW)
        first_ref[:, cols] = p_ref[pl.ds(j, lines, stride=2 * nk), :]
        last_ref[:, cols] = p_ref[pl.ds(nk - tiles + j, lines, stride=2 * nk), :]


def edges(p, nk, width):
    lines = p.shape[0] // (2 * nk)
    return pl.pallas_call(
        functools.partial(edges_kernel, nk),
        in_specs=[VMEM],
        out_specs=[VMEM] * 2,
        out_shape=[jax.ShapeDtypeStruct((lines, width), F32)] * 2,
        compiler_params=pltpu.CompilerParams(vmem_limit_bytes=LIMIT),
        cost_estimate=pl.CostEstimate(flops=8 * 10**9, bytes_accessed=16 * lines * width, transcendentals=0),
        name="edges",
    )(p)


def energy(row, col_ref, pair_ref):
    return row + col_ref[...] - pair_ref[...]


def source_part(p_ref, nk, wide, c):
    lines = p_ref.shape[0] // (2 * nk)
    per = wide // TW
    return jnp.concatenate([p_ref[pl.ds(nk + c * per + j, lines, stride=2 * nk), :] for j in range(per)], 1)


def within(d2_ref, at, xh_ref, xl_ref, kh_ref, kl_ref, cols):
    out = three(dot_nt, xh_ref[...], xl_ref[...], d2_ref[(0, *at)], d2_ref[(1, *at)])
    return out + three(dot_nn, kh_ref[...], kl_ref[...], xh_ref[:, cols], xl_ref[:, cols])


def head_kernel(
    nk, p_ref, d2_ref, kh_ref, kl_ref, row_ref, col_ref, pair_ref, first_ref, last_ref, xh_ref, xl_ref
):
    lines, wide = first_ref.shape
    for k in range(nk):
        cols = slice(k * TW, (k + 1) * TW)
        xh_ref[:, cols], xl_ref[:, cols] = split(p_ref[pl.ds(k, lines, stride=2 * nk), :])
    for c, ref in ((0, first_ref), (nk * TW // wide - 1, last_ref)):
        cols = slice(c * wide, (c + 1) * wide)
        out = within(d2_ref, (cols,), xh_ref, xl_ref, kh_ref, kl_ref, cols) + source_part(p_ref, nk, wide, c)
        ref[...] = out / energy(row_ref[:, cols], col_ref, pair_ref)


def body_kernel(
    nk, p_ref, d2_ref, kh_ref, kl_ref, row_ref, col_ref, pair_ref, first_ref, last_ref, xh_ref, xl_ref,
    o_ref, gh_ref, gl_ref,
):
    lines, wide = first_ref.shape
    count = nk * TW // wide
    for c, ref in ((0, first_ref), (count - 1, last_ref)):
        cols = slice(c * wide, (c + 1) * wide)
        gh_ref[:, cols], gl_ref[:, cols] = split(ref[...])
    for c in range(1, count - 1):
        cols = slice(c * wide, (c + 1) * wide)
        out = within(d2_ref, (cols,), xh_ref, xl_ref, kh_ref, kl_ref, cols) + source_part(p_ref, nk, wide, c)
        gh_ref[:, cols], gl_ref[:, cols] = split(out / energy(row_ref[:, cols], col_ref, pair_ref))
    for c in range(count):
        cols = slice(c * wide, (c + 1) * wide)
        o_ref[:, cols] = within(d2_ref, (cols,), gh_ref, gl_ref, kh_ref, kl_ref, cols) + source_part(p_ref, nk, wide, c)


def mid_kernel(
    t_ref, first_ref, last_ref, before_ref, after_ref, low_ref, high_ref, low_next_ref, high_prev_ref,
    d2_ref, kh_ref, kl_ref, row_ref, row_prev_ref, row_next_ref, col_ref, pair_ref, o_ref,
):
    rows = t_ref.shape[1]
    wide = low_ref.shape[0]
    low = split(low_ref[...])
    high = split(high_ref[...])
    front = slice(0, wide)
    rear = slice(rows - wide, rows)
    own_front = three(dot_nt, *split(before_ref[...]), *low) / energy(row_ref[:, front], col_ref, pair_ref)
    own_rear = three(dot_nt, *split(after_ref[...]), *high) / energy(row_ref[:, rear], col_ref, pair_ref)
    prev = three(dot_nt, *split(first_ref[...]), *split(high_prev_ref[...]))
    prev = prev / energy(row_prev_ref[...], col_ref, pair_ref)
    after = three(dot_nt, *split(last_ref[...]), *split(low_next_ref[...]))
    after = after / energy(row_next_ref[...], col_ref, pair_ref)
    own_front = split(own_front)
    own_rear = split(own_rear)
    count = rows // wide
    for c in range(count):
        cols = slice(c * wide, (c + 1) * wide)
        out = t_ref[:, cols]
        out += three(dot_nt, *own_front, d2_ref[0, cols, front], d2_ref[1, cols, front])
        out += three(dot_nt, *own_rear, d2_ref[0, cols, rear], d2_ref[1, cols, rear])
        if c == 0:
            out += three(dot_nn, kh_ref[...], kl_ref[...], *own_front)
            out += three(dot_nt, *split(prev), *low)
        if c == count - 1:
            out += three(dot_nn, kh_ref[...], kl_ref[...], *own_rear)
            out += three(dot_nt, *split(after), *high)
        o_ref[:, cols] = out


def finish_kernel(nk, t_ref, before_ref, after_ref, low_ref, high_ref, row_ref, col_ref, pair_ref, o_ref):
    lines, rows = t_ref.shape
    wide = low_ref.shape[0]
    count = rows // wide
    per = wide // TW
    for c in [*range(1, count - 1), 0, count - 1]:
        cols = slice(c * wide, (c + 1) * wide)
        out = t_ref[:, cols]
        if c == 0:
            out += three(dot_nt, *split(before_ref[...]), *split(low_ref[...]))
        if c == count - 1:
            out += three(dot_nt, *split(after_ref[...]), *split(high_ref[...]))
        out = out / energy(row_ref[:, cols], col_ref, pair_ref)
        for j in range(per):
            o_ref[pl.ds(c * per + j, lines, stride=nk), :] = out[:, j * TW : (j + 1) * TW]


def call(name, kernel, args, shapes, flops, scratch=()):
    size = sum(a.size * a.dtype.itemsize for a in (*args, *shapes))
    return pl.pallas_call(
        kernel,
        in_specs=[VMEM] * len(args),
        out_specs=[VMEM] * len(shapes),
        out_shape=shapes,
        scratch_shapes=scratch,
        compiler_params=pltpu.CompilerParams(vmem_limit_bytes=LIMIT),
        cost_estimate=pl.CostEstimate(flops=flops, bytes_accessed=size, transcendentals=0),
        name=name,
    )(*args)


def exchange(first, last):
    count = lax.axis_size("virt")
    up = [(i, i + 1) for i in range(count - 1)]
    down = [(j, i) for i, j in up]
    before = lax.ppermute(last, "virt", up)
    after = lax.ppermute(first, "virt", down)
    return before, after


def local(
    amplitudes,
    source,
    diag_block,
    edge_low,
    edge_high,
    hole_coupling,
    pair_energy,
    virt_energy,
    column_tiles,
):
    rows, cols = amplitudes.shape[1:]
    width = edge_low.shape[0]
    pairs = pair_energy.shape[0]
    share = cols // pairs
    nk = rows // TW
    lines = pairs * share

    packed = pack(amplitudes[0], source[0]).reshape(pairs, share * 2 * nk, TW)
    held = lax.all_to_all(packed, "pair", split_axis=0, concat_axis=0, tiled=True)
    held = held.reshape(lines * 2 * nk, TW)

    parts = prep(diag_block, hole_coupling, share)
    high_prev, low_next = exchange(edge_low, edge_high)
    at = lax.axis_index("virt") * rows
    row = lax.dynamic_slice_in_dim(virt_energy, at, rows)[None, :]
    row_prev = lax.dynamic_slice_in_dim(virt_energy, jnp.maximum(at - width, 0), width)[None, :]
    row_next = lax.dynamic_slice_in_dim(
        virt_energy, jnp.minimum(at + rows, virt_energy.shape[0] - width), width
    )[None, :]
    start = lax.axis_index("pair") * share
    tile = lax.dynamic_index_in_dim(column_tiles, start // TW, keepdims=False)
    kept = lax.dynamic_slice_in_dim(virt_energy, tile * TW + start % TW, share)
    col = jnp.broadcast_to(kept[None, :], (pairs, share)).reshape(-1, 1)
    own = jnp.broadcast_to(pair_energy[:, None], (pairs, share)).reshape(-1, 1)
    small = (edge_low, edge_high, low_next, high_prev, row, row_prev, row_next, col, own)
    held, parts, small = lax.optimization_barrier((held, parts, small))
    low, high, low_next, high_prev, row, row_prev, row_next, col, own = small

    full = jax.ShapeDtypeStruct((lines, rows), F32)
    edge = jax.ShapeDtypeStruct((lines, width), F32)
    scratch = [pltpu.VMEM((lines, rows), BF)] * 2
    most = 6 * lines * rows * (rows + lines)
    first, last = edges(held, nk, width)
    before, after = exchange(first, last)
    d2, kh, kl = parts
    common = (held, d2, kh, kl, row, col, own)
    half = jax.ShapeDtypeStruct((lines, rows), BF)
    field_first, field_last, xh, xl = call(
        "head", functools.partial(head_kernel, nk), common, [edge, edge, half, half], most // 2
    )
    field_before, field_after = exchange(field_first, field_last)
    (total,) = call(
        "body",
        functools.partial(body_kernel, nk),
        (*common, field_first, field_last, xh, xl),
        [full],
        most + most // 2,
        scratch,
    )
    (total,) = call(
        "mid",
        mid_kernel,
        (total, first, last, before, after, low, high, low_next, high_prev, d2, kh, kl, row, row_prev, row_next, col, own),
        [full],
        most // 2,
    )
    (out,) = call(
        "finish",
        functools.partial(finish_kernel, nk),
        (total, field_before, field_after, low, high, row, col, own),
        [jax.ShapeDtypeStruct((lines * nk, TW), F32)],
        12 * lines * width * width,
    )
    back = lax.all_to_all(out.reshape(pairs, share * nk, TW), "pair", split_axis=0, concat_axis=0, tiled=True)
    return unpack(back.reshape(lines * nk, TW), rows, cols)[None]


def solution(mesh):
    in_specs = (
        P("pair", "virt", None),
        P("pair", "virt", None),
        P("virt", None),
        P("virt", None),
        P("virt", None),
        P(),
        P(),
        P(),
        P(),
    )
    out_specs = P("pair", "virt", None)
    return jax.shard_map(local, mesh=mesh, in_specs=in_specs, out_specs=out_specs, check_vma=False)
```

```python
import functools

import jax
import jax.numpy as jnp
from jax import lax
from jax.experimental import pallas as pl
from jax.experimental.pallas import tpu as pltpu
from jax.sharding import PartitionSpec as P

TW = 128
BF = jnp.bfloat16
F32 = jnp.float32
VMEM = pl.BlockSpec(memory_space=pltpu.VMEM)
HBM = pl.BlockSpec(memory_space=pltpu.HBM)
LIMIT = 16 * 1024 * 1024


def split(x):
    hi = x.astype(BF)
    return hi, (x - hi.astype(F32)).astype(BF)


def dot_nt(x, w):
    return lax.dot_general(x, w, (((1,), (1,)), ((), ())), preferred_element_type=F32)


def dot_nn(x, w):
    return jnp.dot(x, w, preferred_element_type=F32)


def three(dot, xh, xl, wh, wl):
    return dot(xh, wh) + (dot(xl, wh) + dot(xh, wl))


def pack_kernel(a_hbm, o_hbm, a_ref, o_ref, in_sems, out_sems):
    rows, cols = a_ref.shape
    nk = rows // TW
    tiles = cols // TW
    copies = []
    for t in range(tiles):
        here = (slice(None), slice(t * TW, (t + 1) * TW))
        copies.append(pltpu.make_async_copy(a_hbm.at[here], a_ref.at[here], in_sems.at[t]))
        copies[t].start()
    sent = []
    for t in range(tiles):
        copies[t].wait()
        turn(a_ref, o_ref, t, nk)
        here = slice(t * TW * nk, (t + 1) * TW * nk)
        sent.append(pltpu.make_async_copy(o_ref.at[here, :], o_hbm.at[here, :], out_sems.at[t]))
        sent[t].start()
    for copy in sent:
        copy.wait()


def turn(a_ref, o_ref, t, nk):
    for k in range(nk):
        block = a_ref[k * TW : (k + 1) * TW, t * TW : (t + 1) * TW]
        o_ref[pl.ds(t * TW * nk + k, TW, stride=nk), :] = block.T


def pack(a):
    rows, cols = a.shape
    size = (cols * rows // TW, TW)
    return pl.pallas_call(
        pack_kernel,
        in_specs=[HBM],
        out_specs=HBM,
        out_shape=jax.ShapeDtypeStruct(size, F32),
        scratch_shapes=[pltpu.VMEM((rows, cols), F32), pltpu.VMEM(size, F32)]
        + [pltpu.SemaphoreType.DMA((cols // TW,))] * 2,
        compiler_params=pltpu.CompilerParams(vmem_limit_bytes=60 * 1024 * 1024),
        name="pack",
    )(a)


def prep_kernel(share, d_ref, l_ref, d2_ref, kh_ref, kl_ref):
    d2_ref[0], d2_ref[1] = split(d_ref[...])
    pairs = l_ref.shape[0]
    size = pairs * share
    spread = (
        lax.broadcasted_iota(jnp.int32, (size, pairs), 0) // share
        == lax.broadcasted_iota(jnp.int32, (size, pairs), 1)
    ).astype(F32).astype(BF)
    same = (
        lax.broadcasted_iota(jnp.int32, (size, size), 0) % share
        == lax.broadcasted_iota(jnp.int32, (size, size), 1) % share
    )
    for part, ref in zip(split(l_ref[...]), (kh_ref, kl_ref)):
        tall = dot_nn(spread, part).astype(BF)
        wide = dot_nt(tall, spread)
        ref[...] = jnp.where(same, wide, 0.0).astype(BF)


def prep(d, l, share):
    rows = d.shape[0]
    size = l.shape[0] * share
    return pl.pallas_call(
        functools.partial(prep_kernel, share),
        in_specs=[VMEM] * 2,
        out_specs=[VMEM] * 3,
        out_shape=[jax.ShapeDtypeStruct((2, rows, rows), BF)]
        + [jax.ShapeDtypeStruct((size, size), BF)] * 2,
        compiler_params=pltpu.CompilerParams(vmem_limit_bytes=LIMIT),
        cost_estimate=pl.CostEstimate(
            flops=8 * rows * rows, bytes_accessed=8 * rows * rows, transcendentals=0
        ),
        name="prep",
    )(d, l)


def energy(row, col, pair):
    return row + col - pair


def coupled(d2_ref, xh_ref, xl_ref, rows):
    return three(dot_nn, d2_ref[0, rows, :], d2_ref[1, rows, :], xh_ref[...], xl_ref[...])


def with_edges(c, count, out, low_ref, high_ref, before_ref, after_ref):
    if c == 0:
        out += three(dot_nn, *split(low_ref[...]), *split(before_ref[...]))
    if c == count - 1:
        out += three(dot_nn, *split(high_ref[...]), *split(after_ref[...]))
    return out


def own_kernel(
    nk, x_ref, s_ref, before_ref, after_ref, low_ref, high_ref, d2_ref, virt_ref, kept_ref, pair_ref,
    u_ref, packed_ref, first_ref, last_ref, xh_ref, xl_ref,
):
    rows = x_ref.shape[0]
    wide = low_ref.shape[0]
    count = rows // wide
    xh_ref[...], xl_ref[...] = split(x_ref[...])
    for c in range(count):
        here = slice(c * wide, (c + 1) * wide)
        out = coupled(d2_ref, xh_ref, xl_ref, here) + s_ref[here, :]
        out = with_edges(c, count, out, low_ref, high_ref, before_ref, after_ref)
        out = out / energy(virt_ref[here, :], kept_ref[...], pair_ref[...])
        u_ref[here, :] = out
        if c == 0:
            first_ref[...] = out
        if c == count - 1:
            last_ref[...] = out
    for t in range(x_ref.shape[1] // TW):
        turn(u_ref, packed_ref, t, nk)


def again_kernel(u_ref, s_ref, before_ref, after_ref, low_ref, high_ref, d2_ref, o_ref, xh_ref, xl_ref):
    wide = low_ref.shape[0]
    count = u_ref.shape[0] // wide
    xh_ref[...], xl_ref[...] = split(u_ref[...])
    for c in range(count):
        here = slice(c * wide, (c + 1) * wide)
        out = coupled(d2_ref, xh_ref, xl_ref, here) + s_ref[here, :]
        o_ref[here, :] = with_edges(c, count, out, low_ref, high_ref, before_ref, after_ref)


def ladder_kernel(nk, p_ref, kh_ref, kl_ref, row_ref, col_ref, pair_ref, w_ref, first_ref, last_ref):
    lines = w_ref.shape[0]
    tiles = first_ref.shape[1] // TW
    for k in range(nk):
        cols = slice(k * TW, (k + 1) * TW)
        x = split(p_ref[pl.ds(k, lines, stride=nk), :])
        out = three(dot_nn, kh_ref[...], kl_ref[...], *x)
        out = out / energy(row_ref[:, cols], col_ref[...], pair_ref[...])
        w_ref[:, cols] = out
        if k < tiles:
            first_ref[:, cols] = out
        if k >= nk - tiles:
            j = k - nk + tiles
            last_ref[:, j * TW : (j + 1) * TW] = out


def inner_kernel(wide, w_ref, d2_ref, kh_ref, kl_ref, o_ref, xh_ref, xl_ref):
    xh_ref[...], xl_ref[...] = split(w_ref[...])
    for c in range(w_ref.shape[1] // wide):
        cols = slice(c * wide, (c + 1) * wide)
        out = three(dot_nt, xh_ref[...], xl_ref[...], d2_ref[0, cols, :], d2_ref[1, cols, :])
        o_ref[:, cols] = out + three(dot_nn, kh_ref[...], kl_ref[...], xh_ref[:, cols], xl_ref[:, cols])


def outer_kernel(t_ref, before_ref, after_ref, low_ref, high_ref, o_ref):
    rows = t_ref.shape[1]
    wide = low_ref.shape[0]
    front = slice(0, wide)
    rear = slice(rows - wide, rows)
    o_ref[:, wide : rows - wide] = t_ref[:, wide : rows - wide]
    o_ref[:, front] = t_ref[:, front] + three(dot_nt, *split(before_ref[...]), *split(low_ref[...]))
    o_ref[:, rear] = t_ref[:, rear] + three(dot_nt, *split(after_ref[...]), *split(high_ref[...]))


def join_kernel(nk, p_ref, t_ref, kh_ref, kl_ref, o_ref):
    lines = t_ref.shape[0]
    for k in range(nk):
        here = pl.ds(k, lines, stride=nk)
        x = split(p_ref[here, :])
        o_ref[here, :] = three(dot_nn, kh_ref[...], kl_ref[...], *x) + t_ref[:, k * TW : (k + 1) * TW]


def last_kernel(p_ref, t_ref, virt_ref, kept_ref, pair_ref, o_hbm, o_ref, sems):
    rows, cols = t_ref.shape
    nk = rows // TW
    per = 2
    copies = []
    for k in range(nk):
        here = slice(k * TW, (k + 1) * TW)
        for t in range(cols // TW):
            lanes = slice(t * TW, (t + 1) * TW)
            out = t_ref[here, lanes] + p_ref[pl.ds(t * TW * nk + k, TW, stride=nk), :].T
            o_ref[here, lanes] = out / energy(virt_ref[here, :], kept_ref[:, lanes], pair_ref[...])
        if k % per == per - 1:
            done = slice((k + 1 - per) * TW, (k + 1) * TW)
            copies.append(pltpu.make_async_copy(o_ref.at[done, :], o_hbm.at[done, :], sems.at[k // per]))
            copies[-1].start()
    for copy in copies:
        copy.wait()


def call(name, kernel, args, shapes, flops, scratch=(), out_specs=None):
    size = sum(a.size * a.dtype.itemsize for a in (*args, *shapes))
    return pl.pallas_call(
        kernel,
        in_specs=[VMEM] * len(args),
        out_specs=out_specs or [VMEM] * len(shapes),
        out_shape=shapes,
        scratch_shapes=scratch,
        compiler_params=pltpu.CompilerParams(vmem_limit_bytes=LIMIT),
        cost_estimate=pl.CostEstimate(flops=flops, bytes_accessed=size, transcendentals=0),
        name=name,
    )(*args)


def exchange(first, last):
    count = lax.axis_size("virt")
    up = [(i, i + 1) for i in range(count - 1)]
    down = [(j, i) for i, j in up]
    before = lax.ppermute(last, "virt", up)
    after = lax.ppermute(first, "virt", down)
    return before, after


def local(
    amplitudes,
    source,
    diag_block,
    edge_low,
    edge_high,
    hole_coupling,
    pair_energy,
    virt_energy,
    column_tiles,
):
    rows, cols = amplitudes.shape[1:]
    width = edge_low.shape[0]
    pairs = pair_energy.shape[0]
    share = cols // pairs
    nk = rows // TW
    lines = pairs * share

    def shape(*dims, kind=F32):
        return jax.ShapeDtypeStruct(dims, kind)

    def spread(packed):
        out = lax.all_to_all(packed.reshape(pairs, share * nk, TW), "pair", split_axis=0, concat_axis=0, tiled=True)
        return out.reshape(lines * nk, TW)

    field = amplitudes[0]
    held = spread(pack(field))

    at = lax.axis_index("virt") * rows
    row = lax.dynamic_slice_in_dim(virt_energy, at, rows)
    mine = lax.dynamic_slice_in_dim(pair_energy, lax.axis_index("pair"), 1)
    kept = jnp.concatenate(
        [lax.dynamic_slice_in_dim(virt_energy, column_tiles[t] * TW, TW) for t in range(cols // TW)]
    )
    own_energy = (row[:, None], kept[None, :], mine[None, :])
    start = lax.axis_index("pair") * share
    col = jnp.broadcast_to(lax.dynamic_slice_in_dim(kept, start, share)[None, :], (pairs, share)).reshape(-1, 1)
    all_pairs = jnp.broadcast_to(pair_energy[:, None], (pairs, share)).reshape(-1, 1)
    energies = (row[None, :], col, all_pairs)

    d2, kh, kl = prep(diag_block, hole_coupling, share)
    most = 6 * lines * rows * rows
    pair_scratch = [pltpu.VMEM((rows, cols), BF)] * 2
    before, after = exchange(field[:width], field[rows - width :])
    u, packed, first, last = call(
        "own",
        functools.partial(own_kernel, nk),
        (field, source[0], before, after, edge_low, edge_high, d2, *own_energy),
        [shape(rows, cols), shape(cols * nk, TW), shape(width, cols), shape(width, cols)],
        most,
        pair_scratch,
    )
    held_u = spread(packed)
    u_before, u_after = exchange(first, last)

    w, first, last = call(
        "ladder",
        functools.partial(ladder_kernel, nk),
        (held, kh, kl, *energies),
        [shape(lines, rows), shape(lines, width), shape(lines, width)],
        most // 4,
    )
    before, after = exchange(first, last)
    (total,) = call(
        "inner",
        functools.partial(inner_kernel, width),
        (w, d2, kh, kl),
        [shape(lines, rows)],
        most + most // 4,
        [pltpu.VMEM((lines, rows), BF)] * 2,
    )
    (total,) = call("outer", outer_kernel, (total, before, after, edge_low, edge_high), [shape(lines, rows)], most // 8)
    (out,) = call(
        "join", functools.partial(join_kernel, nk), (held_u, total, kh, kl), [shape(lines * nk, TW)], most // 4
    )
    back = spread(out)
    (own,) = call(
        "again",
        again_kernel,
        (u, source[0], u_before, u_after, edge_low, edge_high, d2),
        [shape(rows, cols)],
        most,
        pair_scratch,
    )
    (out,) = call(
        "last",
        last_kernel,
        (back, own, *own_energy),
        [shape(rows, cols)],
        10 * rows * cols,
        [pltpu.VMEM((rows, cols), F32), pltpu.SemaphoreType.DMA((nk // 2,))],
        [HBM],
    )
    return out[None]


def solution(mesh):
    in_specs = (
        P("pair", "virt", None),
        P("pair", "virt", None),
        P("virt", None),
        P("virt", None),
        P("virt", None),
        P(),
        P(),
        P(),
        P(),
    )
    out_specs = P("pair", "virt", None)
    return jax.shard_map(local, mesh=mesh, in_specs=in_specs, out_specs=out_specs, check_vma=False)
```

```python
import functools

import jax
import jax.numpy as jnp
from jax import lax
from jax.experimental import pallas as pl
from jax.experimental.pallas import tpu as pltpu
from jax.sharding import PartitionSpec as P

TW = 128
BF = jnp.bfloat16
F32 = jnp.float32
VMEM = pl.BlockSpec(memory_space=pltpu.VMEM)
HBM = pl.BlockSpec(memory_space=pltpu.HBM)
LIMIT = 16 * 1024 * 1024


def split(x):
    hi = x.astype(BF)
    return hi, (x - hi.astype(F32)).astype(BF)


def dot_nt(x, w):
    return lax.dot_general(x, w, (((1,), (1,)), ((), ())), preferred_element_type=F32)


def dot_nn(x, w):
    return jnp.dot(x, w, preferred_element_type=F32)


def three(dot, xh, xl, wh, wl):
    return dot(xh, wh) + (dot(xl, wh) + dot(xh, wl))


def pack_kernel(a_hbm, o_hbm, a_ref, o_ref, in_sems, out_sems):
    rows, cols = a_ref.shape
    nk = rows // TW
    tiles = cols // TW
    copies = []
    for t in range(tiles):
        here = (slice(None), slice(t * TW, (t + 1) * TW))
        copies.append(pltpu.make_async_copy(a_hbm.at[here], a_ref.at[here], in_sems.at[t]))
        copies[t].start()
    sent = []
    for t in range(tiles):
        copies[t].wait()
        turn(a_ref, o_ref, t, nk)
        here = slice(t * TW * nk, (t + 1) * TW * nk)
        sent.append(pltpu.make_async_copy(o_ref.at[here, :], o_hbm.at[here, :], out_sems.at[t]))
        sent[t].start()
    for copy in sent:
        copy.wait()


def turn(a_ref, o_ref, t, nk):
    for k in range(nk):
        block = a_ref[k * TW : (k + 1) * TW, t * TW : (t + 1) * TW]
        o_ref[pl.ds(t * TW * nk + k, TW, stride=nk), :] = block.T


def pack(a):
    rows, cols = a.shape
    size = (cols * rows // TW, TW)
    return pl.pallas_call(
        pack_kernel,
        in_specs=[HBM],
        out_specs=HBM,
        out_shape=jax.ShapeDtypeStruct(size, F32),
        scratch_shapes=[pltpu.VMEM((rows, cols), F32), pltpu.VMEM(size, F32)]
        + [pltpu.SemaphoreType.DMA((cols // TW,))] * 2,
        compiler_params=pltpu.CompilerParams(vmem_limit_bytes=60 * 1024 * 1024),
        name="pack",
    )(a)


def prep_kernel(share, l_ref, kh_ref, kl_ref):
    pairs = l_ref.shape[0]
    size = pairs * share
    spread = (
        lax.broadcasted_iota(jnp.int32, (size, pairs), 0) // share
        == lax.broadcasted_iota(jnp.int32, (size, pairs), 1)
    ).astype(F32).astype(BF)
    same = (
        lax.broadcasted_iota(jnp.int32, (size, size), 0) % share
        == lax.broadcasted_iota(jnp.int32, (size, size), 1) % share
    )
    for part, ref in zip(split(l_ref[...]), (kh_ref, kl_ref)):
        tall = dot_nn(spread, part).astype(BF)
        wide = dot_nt(tall, spread)
        ref[...] = jnp.where(same, wide, 0.0).astype(BF)


def energy(row, col, pair):
    return row + col - pair


def with_edges(c, count, out, low_ref, high_ref, before_ref, after_ref):
    if c == 0:
        out += three(dot_nn, *split(low_ref[...]), *split(before_ref[...]))
    if c == count - 1:
        out += three(dot_nn, *split(high_ref[...]), *split(after_ref[...]))
    return out


def own_kernel(
    x_hbm, s_hbm, d_hbm, y_hbm, d2_hbm, x_ref, s_ref, d_ref, xh_ref, xl_ref, d2_ref, y_ref, in_sems, out_sems
):
    rows = x_ref.shape[0]
    count = in_sems.shape[0] - 2
    wide = rows // count
    arrays = [pltpu.make_async_copy(x_hbm, x_ref, in_sems.at[0]), pltpu.make_async_copy(s_hbm, s_ref, in_sems.at[1])]
    arrays[0].start()
    parts = []
    for c in range(count):
        here = slice(c * wide, (c + 1) * wide)
        parts.append(pltpu.make_async_copy(d_hbm.at[here, :], d_ref.at[here, :], in_sems.at[2 + c]))
        parts[c].start()
        if c == 0:
            arrays[1].start()
    sent = []
    arrays[0].wait()
    xh_ref[...], xl_ref[...] = split(x_ref[...])
    for c in range(count):
        here = slice(c * wide, (c + 1) * wide)
        parts[c].wait()
        d2_ref[0, here, :], d2_ref[1, here, :] = split(d_ref[here, :])
        sent.append(pltpu.make_async_copy(d2_ref.at[:, here, :], d2_hbm.at[:, here, :], out_sems.at[0, c]))
        sent[-1].start()
        if c == 0:
            arrays[1].wait()
        out = three(dot_nn, d2_ref[0, here, :], d2_ref[1, here, :], xh_ref[...], xl_ref[...])
        y_ref[here, :] = out + s_ref[here, :]
        sent.append(pltpu.make_async_copy(y_ref.at[here, :], y_hbm.at[here, :], out_sems.at[1, c]))
        sent[-1].start()
    for copy in sent:
        copy.wait()


def ready_kernel(
    nk, y_hbm, before_ref, after_ref, low_ref, high_ref, virt_ref, kept_ref, pair_ref,
    u_hbm, packed_hbm, first_hbm, last_hbm, y_ref, u_ref, packed_ref, in_sems, out_sems,
):
    rows, cols = u_ref.shape
    wide = low_ref.shape[0]
    count = rows // wide
    got = []
    for c in range(count):
        here = slice(c * wide, (c + 1) * wide)
        got.append(pltpu.make_async_copy(y_hbm.at[here, :], y_ref.at[here, :], in_sems.at[c]))
        got[c].start()
    sent = []

    def send(source, target):
        copy = pltpu.make_async_copy(source, target, out_sems.at[len(sent)])
        copy.start()
        sent.append(copy)

    for c in range(count):
        here = slice(c * wide, (c + 1) * wide)
        got[c].wait()
        out = with_edges(c, count, y_ref[here, :], low_ref, high_ref, before_ref, after_ref)
        u_ref[here, :] = out / energy(virt_ref[here, :], kept_ref[...], pair_ref[...])
    for t in range(cols // TW):
        turn(u_ref, packed_ref, t, nk)
        here = slice(t * TW * nk, (t + 1) * TW * nk)
        send(packed_ref.at[here, :], packed_hbm.at[here, :])
    send(u_ref, u_hbm)
    send(u_ref.at[:wide, :], first_hbm)
    send(u_ref.at[rows - wide :, :], last_hbm)
    for copy in sent:
        copy.wait()


def again_kernel(u_ref, s_ref, before_ref, after_ref, low_ref, high_ref, d2_ref, o_ref, xh_ref, xl_ref):
    wide = low_ref.shape[0]
    count = u_ref.shape[0] // wide
    xh_ref[...], xl_ref[...] = split(u_ref[...])
    for c in range(count):
        here = slice(c * wide, (c + 1) * wide)
        out = three(dot_nn, d2_ref[0, here, :], d2_ref[1, here, :], xh_ref[...], xl_ref[...])
        out += s_ref[here, :]
        o_ref[here, :] = with_edges(c, count, out, low_ref, high_ref, before_ref, after_ref)


def ladder_kernel(nk, p_ref, kh_ref, kl_ref, row_ref, col_ref, pair_ref, w_ref, first_ref, last_ref):
    lines = w_ref.shape[0]
    tiles = first_ref.shape[1] // TW
    for k in range(nk):
        cols = slice(k * TW, (k + 1) * TW)
        x = split(p_ref[pl.ds(k, lines, stride=nk), :])
        out = three(dot_nn, kh_ref[...], kl_ref[...], *x)
        out = out / energy(row_ref[:, cols], col_ref[...], pair_ref[...])
        w_ref[:, cols] = out
        if k < tiles:
            first_ref[:, cols] = out
        if k >= nk - tiles:
            j = k - nk + tiles
            last_ref[:, j * TW : (j + 1) * TW] = out


def inner_kernel(wide, w_ref, d2_ref, kh_ref, kl_ref, o_ref, xh_ref, xl_ref):
    xh_ref[...], xl_ref[...] = split(w_ref[...])
    for c in range(w_ref.shape[1] // wide):
        cols = slice(c * wide, (c + 1) * wide)
        out = three(dot_nt, xh_ref[...], xl_ref[...], d2_ref[0, cols, :], d2_ref[1, cols, :])
        o_ref[:, cols] = out + three(dot_nn, kh_ref[...], kl_ref[...], xh_ref[:, cols], xl_ref[:, cols])


def outer_kernel(t_ref, before_ref, after_ref, low_ref, high_ref, o_ref):
    rows = t_ref.shape[1]
    wide = low_ref.shape[0]
    front = slice(0, wide)
    rear = slice(rows - wide, rows)
    o_ref[:, wide : rows - wide] = t_ref[:, wide : rows - wide]
    o_ref[:, front] = t_ref[:, front] + three(dot_nt, *split(before_ref[...]), *split(low_ref[...]))
    o_ref[:, rear] = t_ref[:, rear] + three(dot_nt, *split(after_ref[...]), *split(high_ref[...]))


def join_kernel(nk, share, p_ref, t_ref, l_ref, o_ref, kh_ref, kl_ref):
    prep_kernel(share, l_ref, kh_ref, kl_ref)
    lines = t_ref.shape[0]
    for k in range(nk):
        here = pl.ds(k, lines, stride=nk)
        x = split(p_ref[here, :])
        o_ref[here, :] = three(dot_nn, kh_ref[...], kl_ref[...], *x) + t_ref[:, k * TW : (k + 1) * TW]


def last_kernel(p_ref, t_ref, virt_ref, kept_ref, pair_ref, o_hbm, o_ref, sems):
    rows, cols = t_ref.shape
    nk = rows // TW
    per = 2
    copies = []
    for k in range(nk):
        here = slice(k * TW, (k + 1) * TW)
        for t in range(cols // TW):
            lanes = slice(t * TW, (t + 1) * TW)
            out = t_ref[here, lanes] + p_ref[pl.ds(t * TW * nk + k, TW, stride=nk), :].T
            o_ref[here, lanes] = out / energy(virt_ref[here, :], kept_ref[:, lanes], pair_ref[...])
        if k % per == per - 1:
            done = slice((k + 1 - per) * TW, (k + 1) * TW)
            copies.append(pltpu.make_async_copy(o_ref.at[done, :], o_hbm.at[done, :], sems.at[k // per]))
            copies[-1].start()
    for copy in copies:
        copy.wait()


def call(name, kernel, args, shapes, flops, scratch=(), out_specs=None, hbm=(), limit=LIMIT):
    size = sum(a.size * a.dtype.itemsize for a in (*args, *shapes))
    return pl.pallas_call(
        kernel,
        in_specs=[HBM if i in hbm else VMEM for i in range(len(args))],
        out_specs=out_specs or [VMEM] * len(shapes),
        out_shape=shapes,
        scratch_shapes=scratch,
        compiler_params=pltpu.CompilerParams(vmem_limit_bytes=limit),
        cost_estimate=pl.CostEstimate(flops=flops, bytes_accessed=size, transcendentals=0),
        name=name,
    )(*args)


def exchange(first, last):
    count = lax.axis_size("virt")
    up = [(i, i + 1) for i in range(count - 1)]
    down = [(j, i) for i, j in up]
    before = lax.ppermute(last, "virt", up)
    after = lax.ppermute(first, "virt", down)
    return before, after


def local(
    amplitudes,
    source,
    diag_block,
    edge_low,
    edge_high,
    hole_coupling,
    pair_energy,
    virt_energy,
    column_tiles,
):
    rows, cols = amplitudes.shape[1:]
    width = edge_low.shape[0]
    pairs = pair_energy.shape[0]
    share = cols // pairs
    nk = rows // TW
    lines = pairs * share

    def shape(*dims, kind=F32):
        return jax.ShapeDtypeStruct(dims, kind)

    def spread(packed):
        out = lax.all_to_all(packed.reshape(pairs, share * nk, TW), "pair", split_axis=0, concat_axis=0, tiled=True)
        return out.reshape(lines * nk, TW)

    field = amplitudes[0]
    held = spread(pack(field))

    at = lax.axis_index("virt") * rows
    row = lax.dynamic_slice_in_dim(virt_energy, at, rows)
    mine = lax.dynamic_slice_in_dim(pair_energy, lax.axis_index("pair"), 1)
    kept = jnp.concatenate(
        [lax.dynamic_slice_in_dim(virt_energy, column_tiles[t] * TW, TW) for t in range(cols // TW)]
    )
    own_energy = (row[:, None], kept[None, :], mine[None, :])
    start = lax.axis_index("pair") * share
    col = jnp.broadcast_to(lax.dynamic_slice_in_dim(kept, start, share)[None, :], (pairs, share)).reshape(-1, 1)
    all_pairs = jnp.broadcast_to(pair_energy[:, None], (pairs, share)).reshape(-1, 1)
    energies = (row[None, :], col, all_pairs)

    kh, kl = call(
        "prep", functools.partial(prep_kernel, share), (hole_coupling,), [shape(lines, lines, kind=BF)] * 2, lines**3
    )
    most = 6 * lines * rows * rows
    pair_scratch = [pltpu.VMEM((rows, cols), BF)] * 2
    before, after = exchange(field[:width], field[rows - width :])
    matrix = pltpu.VMEM((rows, cols), F32)
    parts = rows // width
    y, d2 = call(
        "own",
        own_kernel,
        (field, source[0], diag_block),
        [shape(rows, cols), shape(2, rows, rows, kind=BF)],
        most,
        [
            matrix,
            matrix,
            pltpu.VMEM((rows, rows), F32),
            *pair_scratch,
            pltpu.VMEM((2, rows, rows), BF),
            matrix,
            pltpu.SemaphoreType.DMA((2 + parts,)),
            pltpu.SemaphoreType.DMA((2, parts)),
        ],
        [HBM] * 2,
        (0, 1, 2),
        60 * 1024 * 1024,
    )
    u, packed, first, last = call(
        "ready",
        functools.partial(ready_kernel, nk),
        (y, before, after, edge_low, edge_high, *own_energy),
        [shape(rows, cols), shape(cols * nk, TW), shape(width, cols), shape(width, cols)],
        most // 8,
        [
            matrix,
            matrix,
            pltpu.VMEM((cols * nk, TW), F32),
            pltpu.SemaphoreType.DMA((parts,)),
            pltpu.SemaphoreType.DMA((3 + cols // TW,)),
        ],
        [HBM] * 4,
        (0,),
        60 * 1024 * 1024,
    )
    held_u = spread(packed)
    u_before, u_after = exchange(first, last)

    w, first, last = call(
        "ladder",
        functools.partial(ladder_kernel, nk),
        (held, kh, kl, *energies),
        [shape(lines, rows), shape(lines, width), shape(lines, width)],
        most // 4,
    )
    before, after = exchange(first, last)
    (total,) = call(
        "inner",
        functools.partial(inner_kernel, width),
        (w, d2, kh, kl),
        [shape(lines, rows)],
        most + most // 4,
        [pltpu.VMEM((lines, rows), BF)] * 2,
    )
    (total,) = call("outer", outer_kernel, (total, before, after, edge_low, edge_high), [shape(lines, rows)], most // 8)
    (out,) = call(
        "join",
        functools.partial(join_kernel, nk, share),
        (held_u, total, hole_coupling),
        [shape(lines * nk, TW)],
        most // 4,
        [pltpu.VMEM((lines, lines), BF)] * 2,
    )
    back = spread(out)
    (own,) = call(
        "again",
        again_kernel,
        (u, source[0], u_before, u_after, edge_low, edge_high, d2),
        [shape(rows, cols)],
        most,
        pair_scratch,
    )
    (out,) = call(
        "last",
        last_kernel,
        (back, own, *own_energy),
        [shape(rows, cols)],
        10 * rows * cols,
        [pltpu.VMEM((rows, cols), F32), pltpu.SemaphoreType.DMA((nk // 2,))],
        [HBM],
    )
    return out[None]


def solution(mesh):
    in_specs = (
        P("pair", "virt", None),
        P("pair", "virt", None),
        P("virt", None),
        P("virt", None),
        P("virt", None),
        P(),
        P(),
        P(),
        P(),
    )
    out_specs = P("pair", "virt", None)
    return jax.shard_map(local, mesh=mesh, in_specs=in_specs, out_specs=out_specs, check_vma=False)
```

```python
import functools

import jax
import jax.numpy as jnp
from jax import lax
from jax.experimental import pallas as pl
from jax.experimental.pallas import tpu as pltpu
from jax.sharding import PartitionSpec as P

TW = 128
BF = jnp.bfloat16
F32 = jnp.float32
VMEM = pl.BlockSpec(memory_space=pltpu.VMEM)
HBM = pl.BlockSpec(memory_space=pltpu.HBM)
LIMIT = 16 * 1024 * 1024


def split(x):
    hi = x.astype(BF)
    return hi, (x - hi.astype(F32)).astype(BF)


def dot_nt(x, w):
    return lax.dot_general(x, w, (((1,), (1,)), ((), ())), preferred_element_type=F32)


def dot_nn(x, w):
    return jnp.dot(x, w, preferred_element_type=F32)


def three(dot, xh, xl, wh, wl):
    return dot(xh, wh) + (dot(xl, wh) + dot(xh, wl))


def pack_kernel(a_hbm, o_hbm, a_ref, o_ref, in_sems, out_sems):
    rows, cols = a_ref.shape
    nk = rows // TW
    tiles = cols // TW
    copies = []
    for t in range(tiles):
        here = (slice(None), slice(t * TW, (t + 1) * TW))
        copies.append(pltpu.make_async_copy(a_hbm.at[here], a_ref.at[here], in_sems.at[t]))
        copies[t].start()
    sent = []
    for t in range(tiles):
        copies[t].wait()
        turn(a_ref, o_ref, t, nk)
        here = slice(t * TW * nk, (t + 1) * TW * nk)
        sent.append(pltpu.make_async_copy(o_ref.at[here, :], o_hbm.at[here, :], out_sems.at[t]))
        sent[t].start()
    for copy in sent:
        copy.wait()


def turn(a_ref, o_ref, t, nk):
    for k in range(nk):
        block = a_ref[k * TW : (k + 1) * TW, t * TW : (t + 1) * TW]
        o_ref[pl.ds(t * TW * nk + k, TW, stride=nk), :] = block.T


def pack(a):
    rows, cols = a.shape
    size = (cols * rows // TW, TW)
    return pl.pallas_call(
        pack_kernel,
        in_specs=[HBM],
        out_specs=HBM,
        out_shape=jax.ShapeDtypeStruct(size, F32),
        scratch_shapes=[pltpu.VMEM((rows, cols), F32), pltpu.VMEM(size, F32)]
        + [pltpu.SemaphoreType.DMA((cols // TW,))] * 2,
        compiler_params=pltpu.CompilerParams(vmem_limit_bytes=60 * 1024 * 1024),
        name="pack",
    )(a)


def prep_kernel(share, l_ref, kh_ref, kl_ref):
    pairs = l_ref.shape[0]
    size = pairs * share
    spread = (
        lax.broadcasted_iota(jnp.int32, (size, pairs), 0) // share
        == lax.broadcasted_iota(jnp.int32, (size, pairs), 1)
    ).astype(F32).astype(BF)
    same = (
        lax.broadcasted_iota(jnp.int32, (size, size), 0) % share
        == lax.broadcasted_iota(jnp.int32, (size, size), 1) % share
    )
    for part, ref in zip(split(l_ref[...]), (kh_ref, kl_ref)):
        tall = dot_nn(spread, part).astype(BF)
        wide = dot_nt(tall, spread)
        ref[...] = jnp.where(same, wide, 0.0).astype(BF)


def energy(row, col, pair):
    return row + col - pair


def own_energy_of(virt_ref, kept_ref, pair_ref, start, stop):
    rows = [virt_ref[:, k * TW : (k + 1) * TW] for k in range(start, stop)]
    tall = jnp.concatenate([jnp.broadcast_to(row, (TW, TW)).T for row in rows], 0)
    tiles = kept_ref.shape[1] // TW
    kept = [kept_ref[:, t * TW : (t + 1) * TW] for t in range(tiles)]
    return jnp.concatenate([energy(tall, part, pair_ref[...]) for part in kept], 1)


def with_edges(c, count, out, low_ref, high_ref, before_ref, after_ref):
    if c == 0:
        out += three(dot_nn, *split(low_ref[...]), *split(before_ref[...]))
    if c == count - 1:
        out += three(dot_nn, *split(high_ref[...]), *split(after_ref[...]))
    return out


def own_kernel(
    x_hbm, s_hbm, d_hbm, y_hbm, d2_hbm, x_ref, s_ref, d_ref, xh_ref, xl_ref, d2_ref, y_ref, in_sems, out_sems
):
    rows = x_ref.shape[0]
    count = in_sems.shape[0] - 2
    wide = rows // count
    arrays = [pltpu.make_async_copy(x_hbm, x_ref, in_sems.at[0]), pltpu.make_async_copy(s_hbm, s_ref, in_sems.at[1])]
    arrays[0].start()
    parts = []
    for c in range(count):
        here = slice(c * wide, (c + 1) * wide)
        parts.append(pltpu.make_async_copy(d_hbm.at[here, :], d_ref.at[here, :], in_sems.at[2 + c]))
        parts[c].start()
        if c == 0:
            arrays[1].start()
    sent = []
    arrays[0].wait()
    xh_ref[...], xl_ref[...] = split(x_ref[...])
    for c in range(count):
        here = slice(c * wide, (c + 1) * wide)
        parts[c].wait()
        d2_ref[0, here, :], d2_ref[1, here, :] = split(d_ref[here, :])
        sent.append(pltpu.make_async_copy(d2_ref.at[:, here, :], d2_hbm.at[:, here, :], out_sems.at[0, c]))
        sent[-1].start()
        if c == 0:
            arrays[1].wait()
        out = three(dot_nn, d2_ref[0, here, :], d2_ref[1, here, :], xh_ref[...], xl_ref[...])
        y_ref[here, :] = out + s_ref[here, :]
        sent.append(pltpu.make_async_copy(y_ref.at[here, :], y_hbm.at[here, :], out_sems.at[1, c]))
        sent[-1].start()
    for copy in sent:
        copy.wait()


def ready_kernel(
    nk, y_hbm, before_ref, after_ref, low_ref, high_ref, virt_ref, kept_ref, pair_ref,
    u_hbm, packed_hbm, first_hbm, last_hbm, y_ref, u_ref, packed_ref, in_sems, out_sems,
):
    rows, cols = u_ref.shape
    wide = low_ref.shape[0]
    count = rows // wide
    got = []
    for c in range(count):
        here = slice(c * wide, (c + 1) * wide)
        got.append(pltpu.make_async_copy(y_hbm.at[here, :], y_ref.at[here, :], in_sems.at[c]))
        got[c].start()
    sent = []

    def send(source, target):
        copy = pltpu.make_async_copy(source, target, out_sems.at[len(sent)])
        copy.start()
        sent.append(copy)

    for c in range(count):
        here = slice(c * wide, (c + 1) * wide)
        got[c].wait()
        out = with_edges(c, count, y_ref[here, :], low_ref, high_ref, before_ref, after_ref)
        u_ref[here, :] = out / own_energy_of(virt_ref, kept_ref, pair_ref, c * wide // TW, (c + 1) * wide // TW)
    for t in range(cols // TW):
        turn(u_ref, packed_ref, t, nk)
        here = slice(t * TW * nk, (t + 1) * TW * nk)
        send(packed_ref.at[here, :], packed_hbm.at[here, :])
    send(u_ref, u_hbm)
    send(u_ref.at[:wide, :], first_hbm)
    send(u_ref.at[rows - wide :, :], last_hbm)
    for copy in sent:
        copy.wait()


def again_kernel(u_ref, s_ref, before_ref, after_ref, low_ref, high_ref, d2_ref, o_ref, xh_ref, xl_ref):
    wide = low_ref.shape[0]
    count = u_ref.shape[0] // wide
    xh_ref[...], xl_ref[...] = split(u_ref[...])
    for c in range(count):
        here = slice(c * wide, (c + 1) * wide)
        out = three(dot_nn, d2_ref[0, here, :], d2_ref[1, here, :], xh_ref[...], xl_ref[...])
        out += s_ref[here, :]
        o_ref[here, :] = with_edges(c, count, out, low_ref, high_ref, before_ref, after_ref)


def ladder_kernel(nk, p_ref, kh_ref, kl_ref, row_ref, col_ref, pair_ref, w_ref, first_ref, last_ref):
    lines = w_ref.shape[0]
    tiles = first_ref.shape[1] // TW
    for k in range(nk):
        cols = slice(k * TW, (k + 1) * TW)
        x = split(p_ref[pl.ds(k, lines, stride=nk), :])
        out = three(dot_nn, kh_ref[...], kl_ref[...], *x)
        out = out / energy(row_ref[:, cols], col_ref[...], pair_ref[...])
        w_ref[:, cols] = out
        if k < tiles:
            first_ref[:, cols] = out
        if k >= nk - tiles:
            j = k - nk + tiles
            last_ref[:, j * TW : (j + 1) * TW] = out


def inner_kernel(wide, w_ref, d2_ref, kh_ref, kl_ref, o_ref, xh_ref, xl_ref):
    xh_ref[...], xl_ref[...] = split(w_ref[...])
    for c in range(w_ref.shape[1] // wide):
        cols = slice(c * wide, (c + 1) * wide)
        out = three(dot_nt, xh_ref[...], xl_ref[...], d2_ref[0, cols, :], d2_ref[1, cols, :])
        o_ref[:, cols] = out + three(dot_nn, kh_ref[...], kl_ref[...], xh_ref[:, cols], xl_ref[:, cols])


def outer_kernel(t_ref, before_ref, after_ref, low_ref, high_ref, o_ref):
    rows = t_ref.shape[1]
    wide = low_ref.shape[0]
    front = slice(0, wide)
    rear = slice(rows - wide, rows)
    o_ref[:, wide : rows - wide] = t_ref[:, wide : rows - wide]
    o_ref[:, front] = t_ref[:, front] + three(dot_nt, *split(before_ref[...]), *split(low_ref[...]))
    o_ref[:, rear] = t_ref[:, rear] + three(dot_nt, *split(after_ref[...]), *split(high_ref[...]))


def join_kernel(nk, share, p_ref, t_ref, l_ref, o_ref, kh_ref, kl_ref):
    prep_kernel(share, l_ref, kh_ref, kl_ref)
    lines = t_ref.shape[0]
    for k in range(nk):
        here = pl.ds(k, lines, stride=nk)
        x = split(p_ref[here, :])
        o_ref[here, :] = three(dot_nn, kh_ref[...], kl_ref[...], *x) + t_ref[:, k * TW : (k + 1) * TW]


def last_kernel(p_ref, t_ref, virt_ref, kept_ref, pair_ref, o_hbm, o_ref, sems):
    rows, cols = t_ref.shape
    nk = rows // TW
    per = 2
    copies = []
    for k in range(nk):
        here = slice(k * TW, (k + 1) * TW)
        denom = own_energy_of(virt_ref, kept_ref, pair_ref, k, k + 1)
        for t in range(cols // TW):
            lanes = slice(t * TW, (t + 1) * TW)
            out = t_ref[here, lanes] + p_ref[pl.ds(t * TW * nk + k, TW, stride=nk), :].T
            o_ref[here, lanes] = out / denom[:, lanes]
        if k % per == per - 1:
            done = slice((k + 1 - per) * TW, (k + 1) * TW)
            copies.append(pltpu.make_async_copy(o_ref.at[done, :], o_hbm.at[done, :], sems.at[k // per]))
            copies[-1].start()
    for copy in copies:
        copy.wait()


def call(name, kernel, args, shapes, flops, scratch=(), out_specs=None, hbm=(), limit=LIMIT):
    size = sum(a.size * a.dtype.itemsize for a in (*args, *shapes))
    return pl.pallas_call(
        kernel,
        in_specs=[HBM if i in hbm else VMEM for i in range(len(args))],
        out_specs=out_specs or [VMEM] * len(shapes),
        out_shape=shapes,
        scratch_shapes=scratch,
        compiler_params=pltpu.CompilerParams(vmem_limit_bytes=limit),
        cost_estimate=pl.CostEstimate(flops=flops, bytes_accessed=size, transcendentals=0),
        name=name,
    )(*args)


def exchange(first, last):
    count = lax.axis_size("virt")
    up = [(i, i + 1) for i in range(count - 1)]
    down = [(j, i) for i, j in up]
    before = lax.ppermute(last, "virt", up)
    after = lax.ppermute(first, "virt", down)
    return before, after


def local(
    amplitudes,
    source,
    diag_block,
    edge_low,
    edge_high,
    hole_coupling,
    pair_energy,
    virt_energy,
    column_tiles,
):
    rows, cols = amplitudes.shape[1:]
    width = edge_low.shape[0]
    pairs = pair_energy.shape[0]
    share = cols // pairs
    nk = rows // TW
    lines = pairs * share

    def shape(*dims, kind=F32):
        return jax.ShapeDtypeStruct(dims, kind)

    def spread(packed):
        out = lax.all_to_all(packed.reshape(pairs, share * nk, TW), "pair", split_axis=0, concat_axis=0, tiled=True)
        return out.reshape(lines * nk, TW)

    field = amplitudes[0]
    held = spread(pack(field))

    at = lax.axis_index("virt") * rows
    row = lax.dynamic_slice_in_dim(virt_energy, at, rows)
    mine = lax.dynamic_slice_in_dim(pair_energy, lax.axis_index("pair"), 1)
    kept = jnp.concatenate(
        [lax.dynamic_slice_in_dim(virt_energy, column_tiles[t] * TW, TW) for t in range(cols // TW)]
    )
    own_energy = (row[None, :], kept[None, :], mine[None, :])
    start = lax.axis_index("pair") * share
    col = jnp.broadcast_to(lax.dynamic_slice_in_dim(kept, start, share)[None, :], (pairs, share)).reshape(-1, 1)
    all_pairs = jnp.broadcast_to(pair_energy[:, None], (pairs, share)).reshape(-1, 1)
    energies = (row[None, :], col, all_pairs)

    kh, kl = call(
        "prep", functools.partial(prep_kernel, share), (hole_coupling,), [shape(lines, lines, kind=BF)] * 2, lines**3
    )
    most = 6 * lines * rows * rows
    pair_scratch = [pltpu.VMEM((rows, cols), BF)] * 2
    before, after = exchange(field[:width], field[rows - width :])
    matrix = pltpu.VMEM((rows, cols), F32)
    parts = rows // width
    y, d2 = call(
        "own",
        own_kernel,
        (field, source[0], diag_block),
        [shape(rows, cols), shape(2, rows, rows, kind=BF)],
        most,
        [
            matrix,
            matrix,
            pltpu.VMEM((rows, rows), F32),
            *pair_scratch,
            pltpu.VMEM((2, rows, rows), BF),
            matrix,
            pltpu.SemaphoreType.DMA((2 + parts,)),
            pltpu.SemaphoreType.DMA((2, parts)),
        ],
        [HBM] * 2,
        (0, 1, 2),
        60 * 1024 * 1024,
    )
    u, packed, first, last = call(
        "ready",
        functools.partial(ready_kernel, nk),
        (y, before, after, edge_low, edge_high, *own_energy),
        [shape(rows, cols), shape(cols * nk, TW), shape(width, cols), shape(width, cols)],
        most // 8,
        [
            matrix,
            matrix,
            pltpu.VMEM((cols * nk, TW), F32),
            pltpu.SemaphoreType.DMA((parts,)),
            pltpu.SemaphoreType.DMA((3 + cols // TW,)),
        ],
        [HBM] * 4,
        (0,),
        60 * 1024 * 1024,
    )
    held_u = spread(packed)
    u_before, u_after = exchange(first, last)

    w, first, last = call(
        "ladder",
        functools.partial(ladder_kernel, nk),
        (held, kh, kl, *energies),
        [shape(lines, rows), shape(lines, width), shape(lines, width)],
        most // 4,
    )
    before, after = exchange(first, last)
    (total,) = call(
        "inner",
        functools.partial(inner_kernel, width),
        (w, d2, kh, kl),
        [shape(lines, rows)],
        most + most // 4,
        [pltpu.VMEM((lines, rows), BF)] * 2,
    )
    (total,) = call("outer", outer_kernel, (total, before, after, edge_low, edge_high), [shape(lines, rows)], most // 8)
    (out,) = call(
        "join",
        functools.partial(join_kernel, nk, share),
        (held_u, total, hole_coupling),
        [shape(lines * nk, TW)],
        most // 4,
        [pltpu.VMEM((lines, lines), BF)] * 2,
    )
    back = spread(out)
    (own,) = call(
        "again",
        again_kernel,
        (u, source[0], u_before, u_after, edge_low, edge_high, d2),
        [shape(rows, cols)],
        most,
        pair_scratch,
    )
    (out,) = call(
        "last",
        last_kernel,
        (back, own, *own_energy),
        [shape(rows, cols)],
        10 * rows * cols,
        [pltpu.VMEM((rows, cols), F32), pltpu.SemaphoreType.DMA((nk // 2,))],
        [HBM],
    )
    return out[None]


def solution(mesh):
    in_specs = (
        P("pair", "virt", None),
        P("pair", "virt", None),
        P("virt", None),
        P("virt", None),
        P("virt", None),
        P(),
        P(),
        P(),
        P(),
    )
    out_specs = P("pair", "virt", None)
    return jax.shard_map(local, mesh=mesh, in_specs=in_specs, out_specs=out_specs, check_vma=False)
```

```python
import functools

import jax
import jax.numpy as jnp
from jax import lax
from jax.experimental import pallas as pl
from jax.experimental.pallas import tpu as pltpu
from jax.sharding import PartitionSpec as P

TW = 128
BF = jnp.bfloat16
F32 = jnp.float32
VMEM = pl.BlockSpec(memory_space=pltpu.VMEM)
HBM = pl.BlockSpec(memory_space=pltpu.HBM)
LIMIT = 16 * 1024 * 1024


def split(x):
    hi = x.astype(BF)
    return hi, (x - hi.astype(F32)).astype(BF)


def dot_nt(x, w):
    return lax.dot_general(x, w, (((1,), (1,)), ((), ())), preferred_element_type=F32)


def dot_nn(x, w):
    return jnp.dot(x, w, preferred_element_type=F32)


def three(dot, xh, xl, wh, wl):
    return dot(xh, wh) + (dot(xl, wh) + dot(xh, wl))


def pack_kernel(a_hbm, o_hbm, a_ref, o_ref, in_sems, out_sems):
    rows, cols = a_ref.shape
    nk = rows // TW
    tiles = cols // TW
    copies = []
    for t in range(tiles):
        here = (slice(None), slice(t * TW, (t + 1) * TW))
        copies.append(pltpu.make_async_copy(a_hbm.at[here], a_ref.at[here], in_sems.at[t]))
        copies[t].start()
    sent = []
    for t in range(tiles):
        copies[t].wait()
        turn(a_ref, o_ref, t, nk)
        here = slice(t * TW * nk, (t + 1) * TW * nk)
        sent.append(pltpu.make_async_copy(o_ref.at[here, :], o_hbm.at[here, :], out_sems.at[t]))
        sent[t].start()
    for copy in sent:
        copy.wait()


def turn(a_ref, o_ref, t, nk):
    for k in range(nk):
        block = a_ref[k * TW : (k + 1) * TW, t * TW : (t + 1) * TW]
        o_ref[pl.ds(t * TW * nk + k, TW, stride=nk), :] = block.T


def pack(a):
    rows, cols = a.shape
    size = (cols * rows // TW, TW)
    return pl.pallas_call(
        pack_kernel,
        in_specs=[HBM],
        out_specs=HBM,
        out_shape=jax.ShapeDtypeStruct(size, F32),
        scratch_shapes=[pltpu.VMEM((rows, cols), F32), pltpu.VMEM(size, F32)]
        + [pltpu.SemaphoreType.DMA((cols // TW,))] * 2,
        compiler_params=pltpu.CompilerParams(vmem_limit_bytes=60 * 1024 * 1024),
        name="pack",
    )(a)


def prep_kernel(share, l_ref, kh_ref, kl_ref):
    pairs = l_ref.shape[0]
    size = pairs * share
    spread = (
        lax.broadcasted_iota(jnp.int32, (size, pairs), 0) // share
        == lax.broadcasted_iota(jnp.int32, (size, pairs), 1)
    ).astype(F32).astype(BF)
    same = (
        lax.broadcasted_iota(jnp.int32, (size, size), 0) % share
        == lax.broadcasted_iota(jnp.int32, (size, size), 1) % share
    )
    for part, ref in zip(split(l_ref[...]), (kh_ref, kl_ref)):
        tall = dot_nn(spread, part).astype(BF)
        wide = dot_nt(tall, spread)
        ref[...] = jnp.where(same, wide, 0.0).astype(BF)


def energy(row, col, pair):
    return row + col - pair


def own_energy_of(virt_ref, kept_ref, pair_ref, start, stop):
    rows = [virt_ref[:, k * TW : (k + 1) * TW] for k in range(start, stop)]
    tall = jnp.concatenate([jnp.broadcast_to(row, (TW, TW)).T for row in rows], 0)
    tiles = kept_ref.shape[1] // TW
    kept = [kept_ref[:, t * TW : (t + 1) * TW] for t in range(tiles)]
    return jnp.concatenate([energy(tall, part, pair_ref[...]) for part in kept], 1)


def with_edges(c, count, out, low_ref, high_ref, before_ref, after_ref):
    if c == 0:
        out += three(dot_nn, *split(low_ref[...]), *split(before_ref[...]))
    if c == count - 1:
        out += three(dot_nn, *split(high_ref[...]), *split(after_ref[...]))
    return out


def own_kernel(
    x_hbm, s_hbm, d_hbm, y_hbm, d2_hbm, x_ref, s_ref, d_ref, xh_ref, xl_ref, d2_ref, y_ref, in_sems, out_sems
):
    rows = x_ref.shape[0]
    count = in_sems.shape[0] - 2
    wide = rows // count
    arrays = [pltpu.make_async_copy(x_hbm, x_ref, in_sems.at[0]), pltpu.make_async_copy(s_hbm, s_ref, in_sems.at[1])]
    arrays[0].start()
    parts = []
    for c in range(count):
        here = slice(c * wide, (c + 1) * wide)
        parts.append(pltpu.make_async_copy(d_hbm.at[here, :], d_ref.at[here, :], in_sems.at[2 + c]))
        parts[c].start()
        if c == 0:
            arrays[1].start()
    sent = []
    arrays[0].wait()
    xh_ref[...], xl_ref[...] = split(x_ref[...])
    for c in range(count):
        here = slice(c * wide, (c + 1) * wide)
        parts[c].wait()
        d2_ref[0, here, :], d2_ref[1, here, :] = split(d_ref[here, :])
        sent.append(pltpu.make_async_copy(d2_ref.at[:, here, :], d2_hbm.at[:, here, :], out_sems.at[0, c]))
        sent[-1].start()
        if c == 0:
            arrays[1].wait()
        out = three(dot_nn, d2_ref[0, here, :], d2_ref[1, here, :], xh_ref[...], xl_ref[...])
        y_ref[here, :] = out + s_ref[here, :]
        sent.append(pltpu.make_async_copy(y_ref.at[here, :], y_hbm.at[here, :], out_sems.at[1, c]))
        sent[-1].start()
    for copy in sent:
        copy.wait()


def ready_kernel(
    nk, y_hbm, before_ref, after_ref, low_ref, high_ref, virt_ref, kept_ref, pair_ref,
    u_hbm, packed_hbm, first_hbm, last_hbm, y_ref, u_ref, packed_ref, in_sems, out_sems,
):
    rows, cols = u_ref.shape
    wide = low_ref.shape[0]
    count = rows // wide
    got = []
    for c in range(count):
        here = slice(c * wide, (c + 1) * wide)
        got.append(pltpu.make_async_copy(y_hbm.at[here, :], y_ref.at[here, :], in_sems.at[c]))
        got[c].start()
    sent = []

    def send(source, target):
        copy = pltpu.make_async_copy(source, target, out_sems.at[len(sent)])
        copy.start()
        sent.append(copy)

    for c in range(count):
        here = slice(c * wide, (c + 1) * wide)
        got[c].wait()
        out = with_edges(c, count, y_ref[here, :], low_ref, high_ref, before_ref, after_ref)
        u_ref[here, :] = out / own_energy_of(virt_ref, kept_ref, pair_ref, c * wide // TW, (c + 1) * wide // TW)
    for t in range(cols // TW):
        turn(u_ref, packed_ref, t, nk)
        here = slice(t * TW * nk, (t + 1) * TW * nk)
        send(packed_ref.at[here, :], packed_hbm.at[here, :])
    send(u_ref, u_hbm)
    send(u_ref.at[:wide, :], first_hbm)
    send(u_ref.at[rows - wide :, :], last_hbm)
    for copy in sent:
        copy.wait()


def again_kernel(u_ref, s_ref, before_ref, after_ref, low_ref, high_ref, d2_ref, o_ref, xh_ref, xl_ref):
    wide = low_ref.shape[0]
    count = u_ref.shape[0] // wide
    xh_ref[...], xl_ref[...] = split(u_ref[...])
    for c in range(count):
        here = slice(c * wide, (c + 1) * wide)
        out = three(dot_nn, d2_ref[0, here, :], d2_ref[1, here, :], xh_ref[...], xl_ref[...])
        out += s_ref[here, :]
        o_ref[here, :] = with_edges(c, count, out, low_ref, high_ref, before_ref, after_ref)


def ladder_kernel(nk, p_ref, kh_ref, kl_ref, row_ref, col_ref, pair_ref, w_ref, first_ref, last_ref):
    lines = w_ref.shape[0]
    tiles = first_ref.shape[1] // TW
    for k in range(nk):
        cols = slice(k * TW, (k + 1) * TW)
        x = split(p_ref[pl.ds(k, lines, stride=nk), :])
        out = three(dot_nn, kh_ref[...], kl_ref[...], *x)
        out = out / energy(row_ref[:, cols], col_ref[...], pair_ref[...])
        w_ref[:, cols] = out
        if k < tiles:
            first_ref[:, cols] = out
        if k >= nk - tiles:
            j = k - nk + tiles
            last_ref[:, j * TW : (j + 1) * TW] = out


def inner_kernel(wide, w_ref, d2_ref, kh_ref, kl_ref, o_ref, xh_ref, xl_ref):
    xh_ref[...], xl_ref[...] = split(w_ref[...])
    for c in range(w_ref.shape[1] // wide):
        cols = slice(c * wide, (c + 1) * wide)
        out = three(dot_nt, xh_ref[...], xl_ref[...], d2_ref[0, cols, :], d2_ref[1, cols, :])
        o_ref[:, cols] = out + three(dot_nn, kh_ref[...], kl_ref[...], xh_ref[:, cols], xl_ref[:, cols])


def outer_kernel(t_ref, before_ref, after_ref, low_ref, high_ref, o_ref):
    rows = t_ref.shape[1]
    wide = low_ref.shape[0]
    front = slice(0, wide)
    rear = slice(rows - wide, rows)
    o_ref[:, wide : rows - wide] = t_ref[:, wide : rows - wide]
    o_ref[:, front] = t_ref[:, front] + three(dot_nt, *split(before_ref[...]), *split(low_ref[...]))
    o_ref[:, rear] = t_ref[:, rear] + three(dot_nt, *split(after_ref[...]), *split(high_ref[...]))


def join_kernel(nk, share, p_ref, t_ref, l_ref, o_ref, kh_ref, kl_ref):
    prep_kernel(share, l_ref, kh_ref, kl_ref)
    lines = t_ref.shape[0]
    for k in range(nk):
        here = pl.ds(k, lines, stride=nk)
        x = split(p_ref[here, :])
        o_ref[here, :] = three(dot_nn, kh_ref[...], kl_ref[...], *x) + t_ref[:, k * TW : (k + 1) * TW]


def last_kernel(p_ref, t_ref, virt_ref, kept_ref, pair_ref, o_hbm, o_ref, sems):
    rows, cols = t_ref.shape
    nk = rows // TW
    per = 2
    copies = []
    for k in range(nk):
        here = slice(k * TW, (k + 1) * TW)
        denom = own_energy_of(virt_ref, kept_ref, pair_ref, k, k + 1)
        for t in range(cols // TW):
            lanes = slice(t * TW, (t + 1) * TW)
            out = t_ref[here, lanes] + p_ref[pl.ds(t * TW * nk + k, TW, stride=nk), :].T
            o_ref[here, lanes] = out / denom[:, lanes]
        if k % per == per - 1:
            done = slice((k + 1 - per) * TW, (k + 1) * TW)
            copies.append(pltpu.make_async_copy(o_ref.at[done, :], o_hbm.at[done, :], sems.at[k // per]))
            copies[-1].start()
    for copy in copies:
        copy.wait()


def call(name, kernel, args, shapes, flops, scratch=(), out_specs=None, hbm=(), limit=LIMIT):
    size = sum(a.size * a.dtype.itemsize for a in (*args, *shapes))
    return pl.pallas_call(
        kernel,
        in_specs=[HBM if i in hbm else VMEM for i in range(len(args))],
        out_specs=out_specs or [VMEM] * len(shapes),
        out_shape=shapes,
        scratch_shapes=scratch,
        compiler_params=pltpu.CompilerParams(vmem_limit_bytes=limit),
        cost_estimate=pl.CostEstimate(flops=flops, bytes_accessed=size, transcendentals=0),
        name=name,
    )(*args)


def exchange(first, last):
    count = lax.axis_size("virt")
    up = [(i, i + 1) for i in range(count - 1)]
    down = [(j, i) for i, j in up]
    before = lax.ppermute(last, "virt", up)
    after = lax.ppermute(first, "virt", down)
    return before, after


def local(
    amplitudes,
    source,
    diag_block,
    edge_low,
    edge_high,
    hole_coupling,
    pair_energy,
    virt_energy,
    column_tiles,
):
    rows, cols = amplitudes.shape[1:]
    width = edge_low.shape[0]
    pairs = pair_energy.shape[0]
    share = cols // pairs
    nk = rows // TW
    lines = pairs * share

    def shape(*dims, kind=F32):
        return jax.ShapeDtypeStruct(dims, kind)

    def spread(packed):
        out = lax.all_to_all(packed.reshape(pairs, share * nk, TW), "pair", split_axis=0, concat_axis=0, tiled=True)
        return out.reshape(lines * nk, TW)

    field = amplitudes[0]
    held = spread(pack(field))

    at = lax.axis_index("virt") * rows
    row = lax.dynamic_slice_in_dim(virt_energy, at, rows)
    mine = lax.dynamic_slice_in_dim(pair_energy, lax.axis_index("pair"), 1)
    kept = jnp.concatenate(
        [lax.dynamic_slice_in_dim(virt_energy, column_tiles[t] * TW, TW) for t in range(cols // TW)]
    )
    own_energy = (row[None, :], kept[None, :], mine[None, :])
    start = lax.axis_index("pair") * share
    col = jnp.broadcast_to(lax.dynamic_slice_in_dim(kept, start, share)[None, :], (pairs, share)).reshape(-1, 1)
    all_pairs = jnp.broadcast_to(pair_energy[:, None], (pairs, share)).reshape(-1, 1)
    energies = (row[None, :], col, all_pairs)

    kh, kl = call(
        "prep", functools.partial(prep_kernel, share), (hole_coupling,), [shape(lines, lines, kind=BF)] * 2, lines**3
    )
    most = 6 * lines * rows * rows
    pair_scratch = [pltpu.VMEM((rows, cols), BF)] * 2
    before, after = exchange(field[:width], field[rows - width :])
    matrix = pltpu.VMEM((rows, cols), F32)
    parts = rows // width
    y, d2 = call(
        "own",
        own_kernel,
        (field, source[0], diag_block),
        [shape(rows, cols), shape(2, rows, rows, kind=BF)],
        most,
        [
            matrix,
            matrix,
            pltpu.VMEM((rows, rows), F32),
            *pair_scratch,
            pltpu.VMEM((2, rows, rows), BF),
            matrix,
            pltpu.SemaphoreType.DMA((2 + parts,)),
            pltpu.SemaphoreType.DMA((2, parts)),
        ],
        [HBM] * 2,
        (0, 1, 2),
        60 * 1024 * 1024,
    )
    u, packed, first, last = call(
        "ready",
        functools.partial(ready_kernel, nk),
        (y, before, after, edge_low, edge_high, *own_energy),
        [shape(rows, cols), shape(cols * nk, TW), shape(width, cols), shape(width, cols)],
        most // 8,
        [
            matrix,
            matrix,
            pltpu.VMEM((cols * nk, TW), F32),
            pltpu.SemaphoreType.DMA((parts,)),
            pltpu.SemaphoreType.DMA((3 + cols // TW,)),
        ],
        [HBM] * 4,
        (0,),
        52 * 1024 * 1024,
    )
    held_u = spread(packed)
    u_before, u_after = exchange(first, last)

    w, first, last = call(
        "ladder",
        functools.partial(ladder_kernel, nk),
        (held, kh, kl, *energies),
        [shape(lines, rows), shape(lines, width), shape(lines, width)],
        most // 4,
    )
    before, after = exchange(first, last)
    (total,) = call(
        "inner",
        functools.partial(inner_kernel, width),
        (w, d2, kh, kl),
        [shape(lines, rows)],
        most + most // 4,
        [pltpu.VMEM((lines, rows), BF)] * 2,
    )
    (total,) = call("outer", outer_kernel, (total, before, after, edge_low, edge_high), [shape(lines, rows)], most // 8)
    (out,) = call(
        "join",
        functools.partial(join_kernel, nk, share),
        (held_u, total, hole_coupling),
        [shape(lines * nk, TW)],
        most // 4,
        [pltpu.VMEM((lines, lines), BF)] * 2,
    )
    back = spread(out)
    (own,) = call(
        "again",
        again_kernel,
        (u, source[0], u_before, u_after, edge_low, edge_high, d2),
        [shape(rows, cols)],
        most,
        pair_scratch,
    )
    (out,) = call(
        "last",
        last_kernel,
        (back, own, *own_energy),
        [shape(rows, cols)],
        10 * rows * cols,
        [pltpu.VMEM((rows, cols), F32), pltpu.SemaphoreType.DMA((nk // 2,))],
        [HBM],
    )
    return out[None]


def solution(mesh):
    in_specs = (
        P("pair", "virt", None),
        P("pair", "virt", None),
        P("virt", None),
        P("virt", None),
        P("virt", None),
        P(),
        P(),
        P(),
        P(),
    )
    out_specs = P("pair", "virt", None)
    return jax.shard_map(local, mesh=mesh, in_specs=in_specs, out_specs=out_specs, check_vma=False)
```
